32 devices in a mesh: grp: 2 (over x), aux: 16 (over z, y, core).
Axes of the slice: x: 2, y: 2, z: 4, core: 2. Of those that a mesh axis runs over, the one named last changes fastest.
Arguments:
- tiles: float32 [1024, 4, 128, 128], P(('grp', 'aux')), parts along dimension 0, may hold values from -0.8 to 0.8
- tile_owner: int32 [1024, 1], P(('grp', 'aux')), parts along dimension 0, may hold values from 0 to 15; in each aligned block of 32 rows (0 to 31, 32 to 63, ...) at most 4 rows name the same one
- tile_sub: int32 [1024], P(('grp', 'aux')), parts along dimension 0, may hold values from 0 to 1
- tile_cols: int32 [1024], P(('grp', 'aux')), parts along dimension 0, may hold values from 0 to 31
- row_order: int32 [64], P('grp'), parts along dimension 0, may hold values from 0 to 31, each once
- orbitals: float32 [8192, 128], P(('grp', 'aux')), parts along dimension 0, may hold values from -0.5 to 0.5
Outputs:
- exchange_rows: float32 [8192, 128], P(('grp', 'aux')), parts along dimension 0
The draws below stay inside these ranges and needn't reach their ends.
There are 2 independent parts, one for each index of `grp`. The reference program is written for one: setup_inputs(seed, part) draws one part's arguments, and reference() takes and returns one part's arrays. A program takes and returns all parts, laid end to end along the dimension named above; each array names one. Nothing has to cross between parts.
Inputs may be any that keep to these rules, and one draw needn't show every extreme that they name: `tile_owner`: in the rows of one device no owner is named by more than 4 tiles, a bound that some block reaches. Owner o holds the row blocks row_order[o * 2] .. row_order[o * 2 + 1].
All inputs are finite; a program needn't handle non-finite values.
Results may differ from the reference program's by a relative error of at most 0.00011.
Values sent between devices are 32-bit elements; how exact they have to be, the bound alone decides.
No kernel may reach another device: no remote copies, remote signals or barrier semaphores. Data moves between devices by JAX's collectives and lax.ppermute only.
A program may use at most 64 MiB of HBM per device.

```python
import math
import jax
import jax.numpy as jnp
import numpy as np
from jax import lax

TB = 128
NOCC = 128
RB_DEV = 2
AUX_DEV = 4
TILES_DEV = 32
CAP = 4
NB = 32
NAO = 4096
TILES = 512
N_AUX = 16


def place_ends(drawn, own_key, least, top_value):
    longest = drawn.shape.index(max(drawn.shape))
    spots = []
    for shift in (0, 1):
        where = [jax.random.randint(jax.random.fold_in(own_key, axis), (), 0, length) for axis, length in enumerate(drawn.shape)]
        where[longest] = (where[longest] + shift) % drawn.shape[longest]
        spots.append(tuple(where))
    return drawn.at[spots[0]].set(least).at[spots[1]].set(top_value)


def steps_of(rng, extent, shards, low, largest):
    level, own = 1.0, jax.random.fold_in(rng, 6)
    for axis_at, shards_of in shards:
        heights = jnp.exp(jax.random.uniform(jax.random.fold_in(own, axis_at), (shards_of,), jnp.float32, low / len(shards), largest / len(shards)))
        level = level * jnp.repeat(heights, extent[axis_at] // shards_of).reshape([-1 if axis == axis_at else 1 for axis in range(len(extent))])
    return level


def shared_out(key, own, number, rows, number_of, top, bound, slope):
    ranking = jax.random.permutation(key, number_of)
    crowded, usual = portions_of(number_of, rows * top, bound, slope, True), portions_of(number_of, rows * top, bound, slope, False)
    places = jnp.arange(number_of)

    def named(sizes, offset_by):
        used = int((sizes > 0).sum())
        fixed = max(1, used // 4)
        shifted = fixed + (places - fixed + offset_by * (used - fixed)) % max(1, number_of - fixed)
        return jnp.zeros((number_of,), jnp.int32).at[ranking[jnp.where(places < fixed, places, shifted)]].set(jnp.asarray(sizes, jnp.int32))

    sizes = jnp.where(number % 4 == 0, named(crowded, number // 4), named(usual, number - number // 4 - 1))
    mixed = jax.random.permutation(jax.random.fold_in(own, 3), number_of)
    source_of, taker = mixed[0:number_of // 2 * 2:2], mixed[1:number_of // 2 * 2:2]
    margin = jnp.minimum(sizes[source_of] - 1, bound - sizes[taker]) // 2
    margin = jnp.where((source_of == ranking[0]) | (taker == ranking[0]) | (sizes[taker] == 0), 0, jnp.maximum(margin, 0))
    shifted = jax.random.randint(jax.random.fold_in(own, 4), (number_of // 2,), 0, 1 << 20) % (margin + 1)
    sizes = sizes.at[source_of].add(-shifted).at[taker].add(shifted)
    items = jnp.searchsorted(jnp.cumsum(sizes), jnp.arange(rows * top), side="right").astype(jnp.int32)
    grid = items.reshape(top, rows).T
    grid = grid[jax.random.permutation(jax.random.fold_in(own, 1), rows)]
    offset_by = jax.random.randint(jax.random.fold_in(own, 2), (rows, 1), 0, top)
    return jnp.take_along_axis(grid, (jnp.arange(top)[None, :] + offset_by) % top, axis=1)


def portions_of(amount, total, reach, lean, full):
    portions = [(1 << 20) // math.isqrt(standing ** lean) + 1 for standing in range(1, amount + 1)]
    largest = reach if full else min(reach, max(-(-total // amount), total * portions[0] // sum(portions)))
    least = 1 if total - largest >= amount - 1 else 0
    counts, spare = [largest] + [least] * (amount - 1), total - largest - least * (amount - 1)
    while spare > 0:
        candidates = [i for i in range(1, amount) if counts[i] < largest] or [i for i in range(1, amount) if counts[i] < reach]
        mass, left = sum([portions[i] for i in candidates]), spare
        for i in candidates:
            extra = min(reach - counts[i], max(1, left * portions[i] // mass), spare)
            counts[i] = counts[i] + extra
            spare = spare - extra
    return np.array(counts)


def scatter_about(key, dims, width, most, split=(), kind=jnp.bfloat16):
    array = width * jax.random.normal(key, dims, jnp.float32)
    if split:
        array = array * steps_of(key, dims, split, -0.22, 0.18)
    return jnp.clip(array, -most, most).astype(kind)


def setup_inputs(seed: int = 0, part: int = 0) -> dict:
    arg_keys = jax.random.split(jax.random.key(seed), 7)
    part_keys = jax.random.split(jax.random.fold_in(arg_keys[6], part), 7)
    tiles = scatter_about(part_keys[0], (TILES, AUX_DEV, TB, TB), 0.125, 0.8, ((0, 16),), jnp.float32)
    tile_owner_keys = jax.random.split(jax.random.fold_in(part_keys[1], 1), TILES // TILES_DEV)
    tile_owner_turns = jax.random.permutation(jax.random.fold_in(part_keys[1], 3), TILES // TILES_DEV)
    tile_owner = jax.vmap(lambda own, number: shared_out(jax.random.fold_in(part_keys[1], 2), own, number, TILES_DEV, N_AUX, 1, CAP, 2))(tile_owner_keys, tile_owner_turns).reshape((TILES, 1))
    tile_sub = place_ends(jax.random.randint(part_keys[2], (TILES,), 0, RB_DEV), jax.random.fold_in(part_keys[2], 1), 0, RB_DEV - 1).astype(jnp.int32)
    tile_cols = place_ends(jax.random.randint(part_keys[3], (TILES,), 0, NB), jax.random.fold_in(part_keys[3], 1), 0, NB - 1).astype(jnp.int32)
    row_order = jax.random.permutation(part_keys[4], NB).astype(jnp.int32)
    orbitals = scatter_about(part_keys[5], (NAO, NOCC), TB ** -0.5, 0.5, ((0, 16),), jnp.float32)
    return {"tiles": tiles, "tile_owner": tile_owner, "tile_sub": tile_sub, "tile_cols": tile_cols, "row_order": row_order, "orbitals": orbitals}


def reference(tiles, tile_owner, tile_sub, tile_cols, row_order, orbitals):
    highest = lax.Precision.HIGHEST
    blocked = orbitals.reshape(NB, TB, NOCC)
    position = (tile_owner[:, 0] * RB_DEV + tile_sub).astype(jnp.int32)
    row_block = row_order[position]
    keys = jnp.arange(NB, dtype=jnp.int32)

    def one_slab(index, total):
        lower = (index * TILES_DEV).astype(jnp.int32)
        slab = lax.dynamic_slice_in_dim(tiles, lower, TILES_DEV, 0)
        rows = lax.dynamic_slice_in_dim(row_block, lower, TILES_DEV, 0)
        cols = lax.dynamic_slice_in_dim(tile_cols, lower, TILES_DEV, 0)
        places = lax.dynamic_slice_in_dim(position, lower, TILES_DEV, 0)
        half = jnp.einsum("tprl,tlj->tprj", slab, blocked[cols], precision=highest)
        fitted = jnp.einsum("tprj,tri->pji", half, blocked[rows], precision=highest)
        partial_value = jnp.einsum("tprj,pji->tri", half, fitted, precision=highest)
        select = (places[None, :] == keys[:, None]).astype(jnp.float32)
        return total + jnp.einsum("kt,tri->kri", select, partial_value, precision=highest)

    total = lax.fori_loop(0, N_AUX, one_slab, jnp.zeros((NB, TB, NOCC), jnp.float32))
    return total.reshape(NAO, NOCC)
```

```python
import functools

import jax
import jax.numpy as jnp
from jax import lax
from jax.experimental import pallas as pl
from jax.experimental.pallas import tpu as pltpu
from jax.sharding import PartitionSpec as P

F32, BF16 = jnp.float32, jnp.bfloat16
MIB = 1 << 20


def halves(x):
    hi = x.astype(BF16)
    return hi, (x - hi.astype(F32)).astype(BF16)


def dot(a, b):
    return jnp.dot(a, b, preferred_element_type=F32)


def prepare_kernel(per_owner, n_keys, owner_ref, sub_ref, cols_ref, order_ref, tiles_ref,
                   split_ref, tile_ref, slot_ref, first_ref, col_ref, key_ref, row_ref, used_ref, count_ref, buf, sem):
    n_tiles = tiles_ref.shape[0]
    depth, group = buf.shape[0], buf.shape[1]
    steps = n_tiles // group

    def fetch(step, at):
        return pltpu.make_async_copy(tiles_ref.at[pl.ds(step * group, group)], buf.at[at], sem.at[at])

    for step in range(min(depth, steps)):
        fetch(step, step).start()

    def clear(k, _):
        count_ref[k] = 0
        return 0

    lax.fori_loop(0, n_keys, clear, 0)

    def tally(t, _):
        k = owner_ref[t, 0] * per_owner + sub_ref[t]
        count_ref[k] += 1
        slot_ref[t] = 0
        key_ref[t] = 0
        row_ref[t] = 0
        return 0

    lax.fori_loop(0, n_tiles, tally, 0)

    def place(k, carry):
        start, used = carry
        here = count_ref[k]
        count_ref[k] = start

        @pl.when(here > 0)
        def _():
            key_ref[used] = k
            row_ref[used] = order_ref[k]
            slot_ref[start] = 1

        return start + here, used + (here > 0).astype(jnp.int32)

    _, used = lax.fori_loop(0, n_keys, place, (0, 0))
    used_ref[0] = used

    def settle(t, _):
        k = owner_ref[t, 0] * per_owner + sub_ref[t]
        at = count_ref[k]
        count_ref[k] = at + 1
        tile_ref[at] = t
        col_ref[at] = cols_ref[t]
        return 0

    lax.fori_loop(0, n_tiles, settle, 0)

    def number(t, last):
        first_ref[t] = slot_ref[t]
        now = last + slot_ref[t]
        slot_ref[t] = now
        return now

    lax.fori_loop(0, n_tiles, number, -1)

    for step in range(steps):
        at = step % depth
        fetch(step, at).wait()
        for i in range(group):
            hi, lo = halves(buf[at, i].reshape(-1, buf.shape[-1]))
            split_ref[step * group + i, :, : buf.shape[-1]] = hi
            split_ref[step * group + i, :, buf.shape[-1] :] = lo
        if step + depth < steps:
            fetch(step + depth, at).start()


def prepare(tile_owner, tile_sub, tile_cols, row_order, tiles, per_owner):
    n_tiles, aux_dev, block, _ = tiles.shape
    n_keys = row_order.shape[0]
    smem = pl.BlockSpec(memory_space=pltpu.SMEM)
    ints = jax.ShapeDtypeStruct((n_tiles,), jnp.int32)
    return pl.pallas_call(
        functools.partial(prepare_kernel, per_owner, n_keys),
        out_shape=(pltpu.VMEM((n_tiles, aux_dev * block, 2 * block), BF16),) + (ints,) * 6 + (jax.ShapeDtypeStruct((1,), jnp.int32),),
        in_specs=[smem] * 4 + [pl.BlockSpec(memory_space=pl.ANY)],
        out_specs=(pl.BlockSpec(memory_space=pltpu.VMEM),) + (smem,) * 7,
        scratch_shapes=[
            pltpu.SMEM((n_keys,), jnp.int32),
            pltpu.VMEM((4, 2, aux_dev, block, block), F32),
            pltpu.SemaphoreType.DMA((4,)),
        ],
        compiler_params=pltpu.CompilerParams(vmem_limit_bytes=24 * MIB),
        name="prepare",
    )(tile_owner, tile_sub, tile_cols, row_order, tiles)


class Grid:
    def __init__(self, n_aux):
        self.y, self.core = 2, 2
        self.z = n_aux // (self.y * self.core)
        self.offsets = [(k, j, c) for c in range(self.core) for k in range(self.z) for j in range(self.y)]

    def index(self, z, y, core):
        return (z * self.y + y) * self.core + core

    def other(self, me, offset):
        k, j, c = offset
        z, y, core = me // (self.y * self.core), me // self.core % self.y, me % self.core
        return self.index((z + k) % self.z, (y + j) % self.y, (core + c) % self.core)

    def shift(self, x, offset):
        return lax.ppermute(x, "aux", [(i, self.other(i, offset)) for i in range(self.z * self.y * self.core)])

    def back(self, offset):
        return (-offset[0]) % self.z, offset[1], offset[2]


def hops(grid):
    return sorted(range(1, grid.z), key=lambda k: min(k, grid.z - k))


def gather_shards(grid, x):
    held = {(0, 0, 0): x}
    for k in hops(grid):
        held[k, 0, 0] = grid.shift(x, (-k, 0, 0))
    for k in [0] + hops(grid):
        held[k, 1, 0] = grid.shift(held[k, 0, 0], (0, 1, 0))
    for k, j, _ in list(held):
        held[k, j, 1] = grid.shift(held[k, j, 0], (0, 0, 1))
    return [held[o] for o in grid.offsets]


def scatter_sums(grid, parts):
    order = hops(grid)[::-1] + [0]
    crossed = {k: grid.shift(parts[1][k], (0, 0, 1)) for k in order}
    total = {}
    for k in order:
        pair = parts[0][k] + crossed[k]
        total[k] = pair[0] + grid.shift(pair[1], (0, 1, 0))
    out = total[0]
    for k in order[:-1]:
        out = out + grid.shift(total[k], (k, 0, 0))
    return out


def exchange_kernel(grid, per_owner, tile_ref, slot_ref, first_ref, col_ref, key_ref, row_ref, used_ref, split_ref, *refs):
    n_tiles, rows, pair = split_ref.shape
    block = pair // 2
    aux_dev = rows // block
    n_shards = len(grid.offsets) if grid else 1
    shards, refs = refs[:n_shards], refs[n_shards:]
    *outs, coeff, wide, running, fitted, weights, summed = refs
    me = lax.axis_index("aux")
    if grid:
        for ref, offset in zip(shards, grid.offsets):
            coeff[pl.ds(grid.other(me, offset) * per_owner, per_owner)] = ref[...].reshape(per_owner, block, -1)
    else:
        coeff[...] = shards[0][...].reshape(coeff.shape)

    def half_step(t, _):
        c = coeff[col_ref[t]]
        c_hi, c_lo = halves(c)
        top = jnp.concatenate([c_hi, c_lo], axis=1)
        both = dot(split_ref[tile_ref[t]], jnp.concatenate([top, top], axis=0))
        value = both[:, :block] + both[:, block:]
        value = jnp.where(first_ref[t] == 1, value, value + running[...])
        running[...] = value
        hi, lo = halves(value)
        s = slot_ref[t]
        for p in range(aux_dev):
            wide[s, :, p * pair : p * pair + block] = hi[p * block : (p + 1) * block]
            wide[s, :, p * pair + block : (p + 1) * pair] = lo[p * block : (p + 1) * block]
        return 0

    lax.fori_loop(0, n_tiles, half_step, 0)
    used = used_ref[0]
    fitted[...] = jnp.zeros_like(fitted)

    def fit_step(s, _):
        c_hi, c_lo = halves(coeff[row_ref[s]].T)
        left = jnp.concatenate([jnp.concatenate([c_hi, c_hi], axis=1), jnp.concatenate([c_lo, c_lo], axis=1)], axis=0)
        w = wide[s]
        hi = jnp.concatenate([w[:, p * pair : p * pair + block] for p in range(aux_dev)], axis=1)
        lo = jnp.concatenate([w[:, p * pair + block : (p + 1) * pair] for p in range(aux_dev)], axis=1)
        fitted[...] += dot(left, jnp.concatenate([hi, lo], axis=0))
        return 0

    lax.fori_loop(0, used, fit_step, 0)
    for p in range(aux_dev):
        at = pl.ds(p * block, block)
        f_hi, f_lo = halves((fitted[:block, at] + fitted[block:, at]).T)
        both = jnp.concatenate([f_hi, f_lo], axis=1)
        weights[p * pair : p * pair + block, :] = both
        weights[p * pair + block : (p + 1) * pair, :] = both
    if grid:
        summed[...] = jnp.zeros_like(summed)
    else:
        outs[0][...] = jnp.zeros_like(outs[0])

    def out_step(s, _):
        both = dot(wide[s], weights[...])
        value = both[:, :block] + both[:, block:]
        if grid:
            summed[key_ref[s]] = value
        else:
            outs[0][pl.ds(pl.multiple_of(key_ref[s] * block, block), block)] = value
        return 0

    lax.fori_loop(0, used, out_step, 0)
    if grid:
        for c in range(grid.core):
            for k in range(grid.z):
                for j in range(grid.y):
                    at = grid.other(me, (k, j, c)) * per_owner
                    outs[c * grid.z + k][j] = summed[pl.ds(at, per_owner)].reshape(outs[0].shape[1:])


def exchange(grid, meta, split, shards, n_blocks, per_owner):
    n_tiles, rows, pair = split.shape
    block, width = pair // 2, shards[0].shape[1]
    aux_dev = rows // block
    smem = pl.BlockSpec(memory_space=pltpu.SMEM)
    vmem = pl.BlockSpec(memory_space=pltpu.VMEM)
    if grid:
        out_shape = [pltpu.VMEM((grid.y, per_owner * block, width), F32)] * (grid.core * grid.z)
    else:
        out_shape = [jax.ShapeDtypeStruct((n_blocks * block, width), F32)]
    return pl.pallas_call(
        functools.partial(exchange_kernel, grid, per_owner),
        out_shape=out_shape,
        in_specs=[smem] * 7 + [vmem] * (1 + len(shards)),
        out_specs=[vmem] * len(out_shape),
        scratch_shapes=[
            pltpu.VMEM((n_blocks, block, width), F32),
            pltpu.VMEM((n_tiles, block, aux_dev * pair), BF16),
            pltpu.VMEM((rows, width), F32),
            pltpu.VMEM((2 * width, aux_dev * block), F32),
            pltpu.VMEM((aux_dev * pair, 2 * width), BF16),
            pltpu.VMEM((n_blocks if grid else 1, block, width), F32),
        ],
        compiler_params=pltpu.CompilerParams(vmem_limit_bytes=48 * MIB),
        name="exchange",
    )(*meta, split, *shards)


def local(tiles, tile_owner, tile_sub, tile_cols, row_order, orbitals):
    n_aux = lax.axis_size("aux")
    n_blocks = row_order.shape[0]
    per_owner = n_blocks // n_aux
    grid = Grid(n_aux) if n_aux % 4 == 0 and n_aux <= 16 else None
    if grid:
        shards = gather_shards(grid, orbitals)
    else:
        shards = [lax.all_gather(orbitals, "aux", axis=0, tiled=True)]
    split, *meta = prepare(tile_owner, tile_sub, tile_cols, row_order, tiles, per_owner)
    split = pltpu.with_memory_space_constraint(split, pltpu.VMEM)
    outs = exchange(grid, meta, split, shards, n_blocks, per_owner)
    if not grid:
        return lax.psum_scatter(outs[0], "aux", scatter_dimension=0, tiled=True)
    return scatter_sums(grid, [outs[: grid.z], outs[grid.z :]])


def solution(mesh):
    in_specs = (
        P(("grp", "aux"), None, None, None),
        P(("grp", "aux"), None),
        P(("grp", "aux")),
        P(("grp", "aux")),
        P("grp"),
        P(("grp", "aux"), None),
    )
    out_specs = P(("grp", "aux"), None)
    return jax.shard_map(local, mesh=mesh, in_specs=in_specs, out_specs=out_specs, check_vma=False)
```

```python
import functools

import jax
import jax.numpy as jnp
from jax import lax
from jax.experimental import pallas as pl
from jax.experimental.pallas import tpu as pltpu
from jax.sharding import PartitionSpec as P

F32, BF16 = jnp.float32, jnp.bfloat16
MIB = 1 << 20
HALF_UNROLL, FIT, OUT = 16, 16, 16


def halves(x):
    hi = x.astype(BF16)
    return hi, (x - hi.astype(F32)).astype(BF16)


def dot(a, b):
    return jnp.dot(a, b, preferred_element_type=F32)


def prepare_kernel(tiles_ref, split_ref, buf, sem):
    n_tiles = tiles_ref.shape[0]
    depth, group = buf.shape[0], buf.shape[1]
    steps = n_tiles // group

    def fetch(step, at):
        return pltpu.make_async_copy(tiles_ref.at[pl.ds(step * group, group)], buf.at[at], sem.at[at])

    for step in range(min(depth, steps)):
        fetch(step, step).start()
    for step in range(steps):
        at = step % depth
        fetch(step, at).wait()
        for i in range(group):
            hi, lo = halves(buf[at, i].reshape(-1, buf.shape[-1]))
            split_ref[step * group + i, :, : buf.shape[-1]] = hi
            split_ref[step * group + i, :, buf.shape[-1] :] = lo
        if step + depth < steps:
            fetch(step + depth, at).start()


def prepare(tiles):
    n_tiles, aux_dev, block, _ = tiles.shape
    return pl.pallas_call(
        prepare_kernel,
        out_shape=pltpu.VMEM((n_tiles, aux_dev * block, 2 * block), BF16),
        in_specs=[pl.BlockSpec(memory_space=pltpu.HBM)],
        out_specs=pl.BlockSpec(memory_space=pltpu.VMEM),
        scratch_shapes=[
            pltpu.VMEM((4, 2, aux_dev, block, block), F32),
            pltpu.SemaphoreType.DMA((4,)),
        ],
        compiler_params=pltpu.CompilerParams(vmem_limit_bytes=24 * MIB),
        cost_estimate=pl.CostEstimate(flops=6 * tiles.size, bytes_accessed=8 * tiles.size, transcendentals=0),
        name="prepare",
    )(pltpu.with_memory_space_constraint(tiles, pltpu.HBM))


class Grid:
    def __init__(self, n_aux):
        self.y, self.core = 2, 2
        self.z = n_aux // (self.y * self.core)
        self.offsets = [(k, j, c) for c in range(self.core) for k in range(self.z) for j in range(self.y)]

    def index(self, z, y, core):
        return (z * self.y + y) * self.core + core

    def other(self, me, offset):
        k, j, c = offset
        z, y, core = me // (self.y * self.core), me // self.core % self.y, me % self.core
        return self.index((z + k) % self.z, (y + j) % self.y, (core + c) % self.core)

    def shift(self, x, offset):
        return lax.ppermute(x, "aux", [(i, self.other(i, offset)) for i in range(self.z * self.y * self.core)])

    def back(self, offset):
        return (-offset[0]) % self.z, offset[1], offset[2]


def hops(grid):
    return sorted(range(1, grid.z), key=lambda k: min(k, grid.z - k))


def gather_shards(grid, x, beside):
    held = {(0, 0, 0): x}
    for k in hops(grid):
        held[k, 0, 0] = grid.shift(x, (-k, 0, 0))
    first = hops(grid)[0]
    held[first, 0, 0], beside = lax.optimization_barrier((held[first, 0, 0], beside))
    for k in [0] + hops(grid):
        held[k, 1, 0] = grid.shift(held[k, 0, 0], (0, 1, 0))
    for k, j, _ in list(held):
        held[k, j, 1] = grid.shift(held[k, j, 0], (0, 0, 1))
    return [held[o] for o in grid.offsets], beside


def scatter_sums(grid, parts):
    order = hops(grid)[::-1] + [0]
    crossed = {k: grid.shift(parts[1][k], (0, 0, 1)) for k in order}
    total = {}
    for k in order:
        pair = parts[0][k] + crossed[k]
        total[k] = pair[0] + grid.shift(pair[1], (0, 1, 0))
    out = total[0]
    for k in order[:-1]:
        out = out + grid.shift(total[k], (k, 0, 0))
    return out


def exchange_kernel(grid, per_owner, owner_ref, sub_ref, cols_ref, order_ref, split_ref, *refs):
    n_tiles, rows, pair = split_ref.shape
    block = pair // 2
    aux_dev = rows // block
    n_shards = len(grid.offsets) if grid else 1
    shards, refs = refs[:n_shards], refs[n_shards:]
    *outs, coeff, wide, fitted, weights, summed = refs
    me = lax.axis_index("aux")
    if grid:
        for ref, offset in zip(shards, grid.offsets):
            coeff[pl.ds(grid.other(me, offset) * per_owner, per_owner)] = ref[...].reshape(per_owner, block, -1)
    else:
        coeff[...] = shards[0][...].reshape(coeff.shape)

    def position(t):
        return owner_ref[t] * per_owner + sub_ref[t]

    def half_step(t, _):
        c_hi, c_lo = halves(coeff[cols_ref[t]])
        top = jnp.concatenate([c_hi, c_lo], axis=1)
        both = dot(split_ref[t], jnp.concatenate([top, top], axis=0))
        hi, lo = halves(both[:, :block] + both[:, block:])
        for p in range(aux_dev):
            wide[t, :, p * pair : p * pair + block] = hi[p * block : (p + 1) * block]
            wide[t, :, p * pair + block : (p + 1) * pair] = lo[p * block : (p + 1) * block]
        return 0

    lax.fori_loop(0, n_tiles, half_step, 0, unroll=HALF_UNROLL)
    fitted[...] = jnp.zeros_like(fitted)

    def fit_step(step, _):
        left, right = [], []
        for i in range(FIT):
            t = step * FIT + i
            c_hi, c_lo = halves(coeff[order_ref[position(t)]].T)
            left.append(jnp.concatenate([jnp.concatenate([c_hi, c_hi], axis=1), jnp.concatenate([c_lo, c_lo], axis=1)], axis=0))
            w = wide[t]
            right.append(jnp.concatenate([w[:, p * pair : p * pair + block] for p in range(aux_dev)], axis=1))
            right.append(jnp.concatenate([w[:, p * pair + block : (p + 1) * pair] for p in range(aux_dev)], axis=1))
        fitted[...] += dot(jnp.concatenate(left, axis=1), jnp.concatenate(right, axis=0))
        return 0

    lax.fori_loop(0, n_tiles // FIT, fit_step, 0)
    for p in range(aux_dev):
        at = pl.ds(p * block, block)
        f_hi, f_lo = halves((fitted[:block, at] + fitted[block:, at]).T)
        both = jnp.concatenate([f_hi, f_lo], axis=1)
        weights[p * pair : p * pair + block, :] = both
        weights[p * pair + block : (p + 1) * pair, :] = both
    summed[...] = jnp.zeros_like(summed)

    def out_step(step, _):
        both = dot(wide[pl.ds(step * OUT, OUT)].reshape(OUT * block, -1), weights[...])
        value = both[:, :block] + both[:, block:]
        for i in range(OUT):
            summed[position(step * OUT + i)] += value[i * block : (i + 1) * block]
        return 0

    lax.fori_loop(0, n_tiles // OUT, out_step, 0)
    if grid:
        for c in range(grid.core):
            for k in range(grid.z):
                for j in range(grid.y):
                    at = grid.other(me, (k, j, c)) * per_owner
                    outs[c * grid.z + k][j] = summed[pl.ds(at, per_owner)].reshape(outs[0].shape[1:])
    else:
        outs[0][...] = summed[...].reshape(outs[0].shape)


def exchange(grid, tile_owner, tile_sub, tile_cols, row_order, split, shards):
    n_tiles, rows, pair = split.shape
    block, width = pair // 2, shards[0].shape[1]
    aux_dev = rows // block
    n_blocks = row_order.shape[0]
    per_owner = n_blocks // lax.axis_size("aux")
    smem = pl.BlockSpec(memory_space=pltpu.SMEM)
    vmem = pl.BlockSpec(memory_space=pltpu.VMEM)
    if grid:
        out_shape = [pltpu.VMEM((grid.y, per_owner * block, width), F32)] * (grid.core * grid.z)
    else:
        out_shape = [jax.ShapeDtypeStruct((n_blocks * block, width), F32)]
    return pl.pallas_call(
        functools.partial(exchange_kernel, grid, per_owner),
        out_shape=out_shape,
        in_specs=[smem] * 4 + [vmem] * (1 + len(shards)),
        out_specs=[vmem] * len(out_shape),
        scratch_shapes=[
            pltpu.VMEM((n_blocks, block, width), F32),
            pltpu.VMEM((n_tiles, block, aux_dev * pair), BF16),
            pltpu.VMEM((2 * width, aux_dev * block), F32),
            pltpu.VMEM((aux_dev * pair, 2 * width), BF16),
            pltpu.VMEM((n_blocks, block, width), F32),
        ],
        compiler_params=pltpu.CompilerParams(vmem_limit_bytes=(24 if grid else 44) * MIB),
        name="exchange",
    )(tile_owner.reshape(-1), tile_sub, tile_cols, row_order, split, *shards)


def local(tiles, tile_owner, tile_sub, tile_cols, row_order, orbitals):
    n_aux = lax.axis_size("aux")
    grid = Grid(n_aux) if n_aux % 4 == 0 and n_aux <= 16 else None
    split = prepare(tiles)
    if grid:
        shards, split = gather_shards(grid, orbitals, split)
    else:
        shards = [lax.all_gather(orbitals, "aux", axis=0, tiled=True)]
    split = pltpu.with_memory_space_constraint(split, pltpu.VMEM)
    outs = exchange(grid, tile_owner, tile_sub, tile_cols, row_order, split, shards)
    if not grid:
        return lax.psum_scatter(outs[0], "aux", scatter_dimension=0, tiled=True)
    return scatter_sums(grid, [outs[: grid.z], outs[grid.z :]])


def solution(mesh):
    in_specs = (
        P(("grp", "aux"), None, None, None),
        P(("grp", "aux"), None),
        P(("grp", "aux")),
        P(("grp", "aux")),
        P("grp"),
        P(("grp", "aux"), None),
    )
    out_specs = P(("grp", "aux"), None)
    return jax.shard_map(local, mesh=mesh, in_specs=in_specs, out_specs=out_specs, check_vma=False)
```

```python
import functools

import jax
import jax.numpy as jnp
from jax import lax
from jax.experimental import pallas as pl
from jax.experimental.pallas import tpu as pltpu
from jax.sharding import PartitionSpec as P

F32, BF16 = jnp.float32, jnp.bfloat16
MIB = 1 << 20
HALF_UNROLL, FIT, OUT = 16, 16, 16


def halves(x):
    hi = x.astype(BF16)
    return hi, (x - hi.astype(F32)).astype(BF16)


def dot(a, b):
    return jnp.dot(a, b, preferred_element_type=F32)


def prepare_kernel(tiles_ref, split_ref, buf, sem):
    n_tiles = tiles_ref.shape[0]
    depth, group = buf.shape[0], buf.shape[1]
    steps = n_tiles // group

    def fetch(step, at):
        return pltpu.make_async_copy(tiles_ref.at[pl.ds(step * group, group)], buf.at[at], sem.at[at])

    for step in range(min(depth, steps)):
        fetch(step, step).start()
    for step in range(steps):
        at = step % depth
        fetch(step, at).wait()
        for i in range(group):
            hi, lo = halves(buf[at, i].reshape(-1, buf.shape[-1]))
            split_ref[step * group + i, :, : buf.shape[-1]] = hi
            split_ref[step * group + i, :, buf.shape[-1] :] = lo
        if step + depth < steps:
            fetch(step + depth, at).start()


def prepare(tiles):
    n_tiles, aux_dev, block, _ = tiles.shape
    return pl.pallas_call(
        prepare_kernel,
        out_shape=pltpu.VMEM((n_tiles, aux_dev * block, 2 * block), BF16),
        in_specs=[pl.BlockSpec(memory_space=pltpu.HBM)],
        out_specs=pl.BlockSpec(memory_space=pltpu.VMEM),
        scratch_shapes=[
            pltpu.VMEM((4, 2, aux_dev, block, block), F32),
            pltpu.SemaphoreType.DMA((4,)),
        ],
        compiler_params=pltpu.CompilerParams(vmem_limit_bytes=24 * MIB),
        cost_estimate=pl.CostEstimate(flops=6 * tiles.size, bytes_accessed=8 * tiles.size, transcendentals=0),
        name="prepare",
    )(pltpu.with_memory_space_constraint(tiles, pltpu.HBM))


def tie(x, *others):
    x, *others = lax.optimization_barrier((x, *others))
    return x, others


class Grid:
    def __init__(self, n_aux):
        self.y, self.core = 2, 2
        self.z = n_aux // (self.y * self.core)
        self.offsets = [(k, j, c) for c in range(self.core) for k in range(self.z) for j in range(self.y)]

    def other(self, me, offset):
        k, j, c = offset
        return me ^ ((k * self.y + j) * self.core + c)

    def shift(self, x, offset):
        return lax.ppermute(x, "aux", [(i, self.other(i, offset)) for i in range(self.z * self.y * self.core)])


def gather_shards(grid, x, beside):
    held = {(0, 0, 0): x}
    held[3, 0, 0] = grid.shift(x, (3, 0, 0))
    held[1, 0, 0] = grid.shift(x, (1, 0, 0))
    held[0, 1, 0] = grid.shift(x, (0, 1, 0))
    held[3, 0, 0], (beside, held[1, 0, 0]) = tie(held[3, 0, 0], beside, held[1, 0, 0])
    held[2, 0, 0] = grid.shift(held[3, 0, 0], (1, 0, 0))
    for k in (3, 1, 2):
        held[k, 1, 0] = grid.shift(held[k, 0, 0], (0, 1, 0))
    for k, j, _ in list(held):
        held[k, j, 1] = grid.shift(held[k, j, 0], (0, 0, 1))
    return [held[o] for o in grid.offsets], beside


def scatter_sums(grid, parts):
    crossed = {k: grid.shift(parts[1][k], (0, 0, 1)) for k in (2, 1, 3, 0)}
    pairs = {k: parts[0][k] + crossed[k] for k in (2, 1, 3, 0)}
    total = {k: pairs[k][0] + grid.shift(pairs[k][1], (0, 1, 0)) for k in (2, 1, 3)}
    got = {k: grid.shift(total[k], (k, 0, 0)) for k in (2, 1, 3)}
    last, (got[2],) = tie(pairs[0][1], got[2])
    out = pairs[0][0] + grid.shift(last, (0, 1, 0))
    return out + got[2] + got[1] + got[3]


def exchange_kernel(grid, per_owner, owner_ref, sub_ref, cols_ref, order_ref, split_ref, *refs):
    n_tiles, rows, pair = split_ref.shape
    block = pair // 2
    aux_dev = rows // block
    n_shards = len(grid.offsets) if grid else 1
    shards, refs = refs[:n_shards], refs[n_shards:]
    *outs, coeff, wide, fitted, weights, summed = refs
    me = lax.axis_index("aux")
    if grid:
        for ref, offset in zip(shards, grid.offsets):
            coeff[pl.ds(grid.other(me, offset) * per_owner, per_owner)] = ref[...].reshape(per_owner, block, -1)
    else:
        coeff[...] = shards[0][...].reshape(coeff.shape)

    def position(t):
        return owner_ref[t] * per_owner + sub_ref[t]

    def half_step(t, _):
        c_hi, c_lo = halves(coeff[cols_ref[t]])
        top = jnp.concatenate([c_hi, c_lo], axis=1)
        both = dot(split_ref[t], jnp.concatenate([top, top], axis=0))
        hi, lo = halves(both[:, :block] + both[:, block:])
        for p in range(aux_dev):
            wide[t, :, p * pair : p * pair + block] = hi[p * block : (p + 1) * block]
            wide[t, :, p * pair + block : (p + 1) * pair] = lo[p * block : (p + 1) * block]
        return 0

    lax.fori_loop(0, n_tiles, half_step, 0, unroll=HALF_UNROLL)
    fitted[...] = jnp.zeros_like(fitted)

    def fit_step(step, _):
        left, right = [], []
        for i in range(FIT):
            t = step * FIT + i
            c_hi, c_lo = halves(coeff[order_ref[position(t)]].T)
            left.append(jnp.concatenate([jnp.concatenate([c_hi, c_hi], axis=1), jnp.concatenate([c_lo, c_lo], axis=1)], axis=0))
            w = wide[t]
            right.append(jnp.concatenate([w[:, p * pair : p * pair + block] for p in range(aux_dev)], axis=1))
            right.append(jnp.concatenate([w[:, p * pair + block : (p + 1) * pair] for p in range(aux_dev)], axis=1))
        fitted[...] += dot(jnp.concatenate(left, axis=1), jnp.concatenate(right, axis=0))
        return 0

    lax.fori_loop(0, n_tiles // FIT, fit_step, 0)
    for p in range(aux_dev):
        at = pl.ds(p * block, block)
        f_hi, f_lo = halves((fitted[:block, at] + fitted[block:, at]).T)
        both = jnp.concatenate([f_hi, f_lo], axis=1)
        weights[p * pair : p * pair + block, :] = both
        weights[p * pair + block : (p + 1) * pair, :] = both
    summed[...] = jnp.zeros_like(summed)

    def out_step(step, _):
        both = dot(wide[pl.ds(step * OUT, OUT)].reshape(OUT * block, -1), weights[...])
        value = both[:, :block] + both[:, block:]
        for i in range(OUT):
            summed[position(step * OUT + i)] += value[i * block : (i + 1) * block]
        return 0

    lax.fori_loop(0, n_tiles // OUT, out_step, 0)
    if grid:
        for c in range(grid.core):
            for k in range(grid.z):
                for j in range(grid.y):
                    at = grid.other(me, (k, j, c)) * per_owner
                    outs[c * grid.z + k][j] = summed[pl.ds(at, per_owner)].reshape(outs[0].shape[1:])
    else:
        outs[0][...] = summed[...].reshape(outs[0].shape)


def exchange(grid, tile_owner, tile_sub, tile_cols, row_order, split, shards):
    n_tiles, rows, pair = split.shape
    block, width = pair // 2, shards[0].shape[1]
    aux_dev = rows // block
    n_blocks = row_order.shape[0]
    per_owner = n_blocks // lax.axis_size("aux")
    smem = pl.BlockSpec(memory_space=pltpu.SMEM)
    vmem = pl.BlockSpec(memory_space=pltpu.VMEM)
    if grid:
        out_shape = [pltpu.VMEM((grid.y, per_owner * block, width), F32)] * (grid.core * grid.z)
    else:
        out_shape = [jax.ShapeDtypeStruct((n_blocks * block, width), F32)]
    return pl.pallas_call(
        functools.partial(exchange_kernel, grid, per_owner),
        out_shape=out_shape,
        in_specs=[smem] * 4 + [vmem] * (1 + len(shards)),
        out_specs=[vmem] * len(out_shape),
        scratch_shapes=[
            pltpu.VMEM((n_blocks, block, width), F32),
            pltpu.VMEM((n_tiles, block, aux_dev * pair), BF16),
            pltpu.VMEM((2 * width, aux_dev * block), F32),
            pltpu.VMEM((aux_dev * pair, 2 * width), BF16),
            pltpu.VMEM((n_blocks, block, width), F32),
        ],
        compiler_params=pltpu.CompilerParams(vmem_limit_bytes=(24 if grid else 44) * MIB),
        name="exchange",
    )(tile_owner.reshape(-1), tile_sub, tile_cols, row_order, split, *shards)


def local(tiles, tile_owner, tile_sub, tile_cols, row_order, orbitals):
    n_aux = lax.axis_size("aux")
    grid = Grid(n_aux) if n_aux == 16 else None
    split = prepare(tiles)
    if grid:
        shards, split = gather_shards(grid, orbitals, split)
    else:
        shards = [lax.all_gather(orbitals, "aux", axis=0, tiled=True)]
    split = pltpu.with_memory_space_constraint(split, pltpu.VMEM)
    outs = exchange(grid, tile_owner, tile_sub, tile_cols, row_order, split, shards)
    if not grid:
        return lax.psum_scatter(outs[0], "aux", scatter_dimension=0, tiled=True)
    return scatter_sums(grid, [outs[: grid.z], outs[grid.z :]])


def solution(mesh):
    in_specs = (
        P(("grp", "aux"), None, None, None),
        P(("grp", "aux"), None),
        P(("grp", "aux")),
        P(("grp", "aux")),
        P("grp"),
        P(("grp", "aux"), None),
    )
    out_specs = P(("grp", "aux"), None)
    return jax.shard_map(local, mesh=mesh, in_specs=in_specs, out_specs=out_specs, check_vma=False)
```

```python
import functools

import jax
import jax.numpy as jnp
from jax import lax
from jax.experimental import pallas as pl
from jax.experimental.pallas import tpu as pltpu
from jax.sharding import PartitionSpec as P

F32, BF16 = jnp.float32, jnp.bfloat16
MIB = 1 << 20


def halves(x):
    hi = x.astype(BF16)
    return hi, (x - hi.astype(F32)).astype(BF16)


def dot(a, b):
    return jnp.dot(a, b, preferred_element_type=F32)


def prepare_kernel(tiles_ref, split_ref, buf, sem):
    n_tiles = tiles_ref.shape[0]
    depth, group = buf.shape[0], buf.shape[1]
    steps = n_tiles // group

    def fetch(step, at):
        return pltpu.make_async_copy(tiles_ref.at[pl.ds(step * group, group)], buf.at[at], sem.at[at])

    for step in range(min(depth, steps)):
        fetch(step, step).start()
    for step in range(steps):
        at = step % depth
        fetch(step, at).wait()
        for i in range(group):
            hi, lo = halves(buf[at, i].reshape(-1, buf.shape[-1]))
            split_ref[step * group + i, :, : buf.shape[-1]] = hi
            split_ref[step * group + i, :, buf.shape[-1] :] = lo
        if step + depth < steps:
            fetch(step + depth, at).start()


def prepare(tiles):
    n_tiles, aux_dev, block, _ = tiles.shape
    return pl.pallas_call(
        prepare_kernel,
        out_shape=pltpu.VMEM((n_tiles, aux_dev * block, 2 * block), BF16),
        in_specs=[pl.BlockSpec(memory_space=pltpu.HBM)],
        out_specs=pl.BlockSpec(memory_space=pltpu.VMEM),
        scratch_shapes=[
            pltpu.VMEM((4, 2, aux_dev, block, block), F32),
            pltpu.SemaphoreType.DMA((4,)),
        ],
        compiler_params=pltpu.CompilerParams(vmem_limit_bytes=24 * MIB),
        cost_estimate=pl.CostEstimate(flops=6 * tiles.size, bytes_accessed=8 * tiles.size, transcendentals=0),
        name="prepare",
    )(pltpu.with_memory_space_constraint(tiles, pltpu.HBM))


def tie(x, *others):
    x, *others = lax.optimization_barrier((x, *others))
    return x, others


class Grid:
    def __init__(self, n_aux):
        self.y, self.core = 2, 2
        self.z = n_aux // (self.y * self.core)
        self.offsets = [(k, j, c) for c in range(self.core) for k in range(self.z) for j in range(self.y)]

    def other(self, me, offset):
        k, j, c = offset
        return me ^ ((k * self.y + j) * self.core + c)

    def shift(self, x, offset):
        return lax.ppermute(x, "aux", [(i, self.other(i, offset)) for i in range(self.z * self.y * self.core)])


def gather_shards(grid, x, beside):
    held = {(0, 0, 0): x}
    held[3, 0, 0] = grid.shift(x, (3, 0, 0))
    held[1, 0, 0] = grid.shift(x, (1, 0, 0))
    held[0, 1, 0] = grid.shift(x, (0, 1, 0))
    held[3, 0, 0], (beside, held[1, 0, 0]) = tie(held[3, 0, 0], beside, held[1, 0, 0])
    held[3, 1, 0] = grid.shift(held[3, 0, 0], (0, 1, 0))
    held[2, 0, 0] = grid.shift(held[3, 0, 0], (1, 0, 0))
    held[3, 1, 0], (held[1, 0, 0],) = tie(held[3, 1, 0], held[1, 0, 0])
    held[2, 1, 0] = grid.shift(held[3, 1, 0], (1, 0, 0))
    held[1, 1, 0] = grid.shift(held[1, 0, 0], (0, 1, 0))
    for k, j, _ in list(held):
        held[k, j, 1] = grid.shift(held[k, j, 0], (0, 0, 1))
    return [held[o] for o in grid.offsets], beside


def scatter_sums(grid, parts):
    crossed = {k: grid.shift(parts[1][k], (0, 0, 1)) for k in (2, 3, 1, 0)}
    pairs = {k: parts[0][k] + crossed[k] for k in (2, 3, 1, 0)}
    far_away = grid.shift(pairs[2][1], (1, 0, 0))
    far_here, (far_away,) = tie(pairs[2][0], far_away)
    far_here = grid.shift(far_here, (1, 0, 0))
    near = pairs[1][0] + grid.shift(pairs[1][1], (0, 1, 0))
    mirror = grid.shift(pairs[3][1] + far_away, (0, 1, 0))
    own, (mirror,) = tie(pairs[0][1], mirror)
    mirror = pairs[3][0] + far_here + mirror
    own = pairs[0][0] + grid.shift(own, (0, 1, 0))
    return own + grid.shift(near, (1, 0, 0)) + grid.shift(mirror, (3, 0, 0))


def exchange_kernel(grid, per_owner, owner_ref, sub_ref, cols_ref, order_ref, split_ref, *refs):
    n_tiles, rows, pair = split_ref.shape
    block = pair // 2
    aux_dev = rows // block
    n_shards = len(grid.offsets) if grid else 1
    shards, refs = refs[:n_shards], refs[n_shards:]
    *outs, coeff, wide, fitted, weights, summed = refs
    me = lax.axis_index("aux")
    if grid:
        for ref, offset in zip(shards, grid.offsets):
            coeff[pl.ds(grid.other(me, offset) * per_owner, per_owner)] = ref[...].reshape(per_owner, block, -1)
    else:
        coeff[...] = shards[0][...].reshape(coeff.shape)

    def position(t):
        return owner_ref[t] * per_owner + sub_ref[t]

    def half_step(t, _):
        c_hi, c_lo = halves(coeff[cols_ref[t]])
        top = jnp.concatenate([c_hi, c_lo], axis=1)
        both = dot(split_ref[t], jnp.concatenate([top, top], axis=0))
        hi, lo = halves(both[:, :block] + both[:, block:])
        for p in range(aux_dev):
            wide[t, :, p * pair : p * pair + block] = hi[p * block : (p + 1) * block]
            wide[t, :, p * pair + block : (p + 1) * pair] = lo[p * block : (p + 1) * block]
        return 0

    lax.fori_loop(0, n_tiles, half_step, 0, unroll=True)
    left, right_hi, right_lo = [], [], []
    for t in range(n_tiles):
        c_hi, c_lo = halves(coeff[order_ref[position(t)]].T)
        left.append(jnp.concatenate([c_hi, c_lo], axis=0))
        w = wide[t]
        right_hi.append(jnp.concatenate([w[:, p * pair : p * pair + block] for p in range(aux_dev)], axis=1))
        right_lo.append(jnp.concatenate([w[:, p * pair + block : (p + 1) * pair] for p in range(aux_dev)], axis=1))
    left = jnp.concatenate(left, axis=1)
    fitted[...] = dot(left, jnp.concatenate(right_hi, axis=0))
    fitted[:block, :] += dot(left[:block], jnp.concatenate(right_lo, axis=0))
    for p in range(aux_dev):
        at = pl.ds(p * block, block)
        f_hi, f_lo = halves((fitted[:block, at] + fitted[block:, at]).T)
        both = jnp.concatenate([f_hi, f_lo], axis=1)
        weights[p * pair : p * pair + block, :] = both
        weights[p * pair + block : (p + 1) * pair, :] = both
    summed[...] = jnp.zeros_like(summed)

    both = dot(wide[...].reshape(n_tiles * block, -1), weights[...])
    value = both[:, :block] + both[:, block:]
    for t in range(n_tiles):
        summed[position(t)] += value[t * block : (t + 1) * block]
    if grid:
        for c in range(grid.core):
            for k in range(grid.z):
                for j in range(grid.y):
                    at = grid.other(me, (k, j, c)) * per_owner
                    outs[c * grid.z + k][j] = summed[pl.ds(at, per_owner)].reshape(outs[0].shape[1:])
    else:
        outs[0][...] = summed[...].reshape(outs[0].shape)


def exchange(grid, tile_owner, tile_sub, tile_cols, row_order, split, shards):
    n_tiles, rows, pair = split.shape
    block, width = pair // 2, shards[0].shape[1]
    aux_dev = rows // block
    n_blocks = row_order.shape[0]
    per_owner = n_blocks // lax.axis_size("aux")
    smem = pl.BlockSpec(memory_space=pltpu.SMEM)
    vmem = pl.BlockSpec(memory_space=pltpu.VMEM)
    if grid:
        out_shape = [pltpu.VMEM((grid.y, per_owner * block, width), F32)] * (grid.core * grid.z)
    else:
        out_shape = [jax.ShapeDtypeStruct((n_blocks * block, width), F32)]
    return pl.pallas_call(
        functools.partial(exchange_kernel, grid, per_owner),
        out_shape=out_shape,
        in_specs=[smem] * 4 + [vmem] * (1 + len(shards)),
        out_specs=[vmem] * len(out_shape),
        scratch_shapes=[
            pltpu.VMEM((n_blocks, block, width), F32),
            pltpu.VMEM((n_tiles, block, aux_dev * pair), BF16),
            pltpu.VMEM((2 * width, aux_dev * block), F32),
            pltpu.VMEM((aux_dev * pair, 2 * width), BF16),
            pltpu.VMEM((n_blocks, block, width), F32),
        ],
        compiler_params=pltpu.CompilerParams(vmem_limit_bytes=(24 if grid else 44) * MIB),
        name="exchange",
    )(tile_owner.reshape(-1), tile_sub, tile_cols, row_order, split, *shards)


def local(tiles, tile_owner, tile_sub, tile_cols, row_order, orbitals):
    n_aux = lax.axis_size("aux")
    grid = Grid(n_aux) if n_aux == 16 else None
    split = prepare(tiles)
    if grid:
        shards, split = gather_shards(grid, orbitals, split)
    else:
        shards = [lax.all_gather(orbitals, "aux", axis=0, tiled=True)]
    split = pltpu.with_memory_space_constraint(split, pltpu.VMEM)
    outs = exchange(grid, tile_owner, tile_sub, tile_cols, row_order, split, shards)
    if not grid:
        return lax.psum_scatter(outs[0], "aux", scatter_dimension=0, tiled=True)
    return scatter_sums(grid, [outs[: grid.z], outs[grid.z :]])


def solution(mesh):
    in_specs = (
        P(("grp", "aux"), None, None, None),
        P(("grp", "aux"), None),
        P(("grp", "aux")),
        P(("grp", "aux")),
        P("grp"),
        P(("grp", "aux"), None),
    )
    out_specs = P(("grp", "aux"), None)
    return jax.shard_map(local, mesh=mesh, in_specs=in_specs, out_specs=out_specs, check_vma=False)
```

```python
import functools

import jax
import jax.numpy as jnp
from jax import lax
from jax.experimental import pallas as pl
from jax.experimental.pallas import tpu as pltpu
from jax.sharding import PartitionSpec as P

F32, BF16 = jnp.float32, jnp.bfloat16
MIB = 1 << 20


def halves(x):
    hi = x.astype(BF16)
    return hi, (x - hi.astype(F32)).astype(BF16)


def dot(a, b):
    return jnp.dot(a, b, preferred_element_type=F32)


def prepare_kernel(tiles_ref, split_ref, buf, sem):
    n_tiles = tiles_ref.shape[0]
    depth, group = buf.shape[0], buf.shape[1]
    steps = n_tiles // group

    def fetch(step, at):
        return pltpu.make_async_copy(tiles_ref.at[pl.ds(step * group, group)], buf.at[at], sem.at[at])

    for step in range(min(depth, steps)):
        fetch(step, step).start()
    for step in range(steps):
        at = step % depth
        fetch(step, at).wait()
        for i in range(group):
            hi, lo = halves(buf[at, i].reshape(-1, buf.shape[-1]))
            split_ref[step * group + i, :, : buf.shape[-1]] = hi
            split_ref[step * group + i, :, buf.shape[-1] :] = lo
        if step + depth < steps:
            fetch(step + depth, at).start()


def prepare(tiles):
    n_tiles, aux_dev, block, _ = tiles.shape
    return pl.pallas_call(
        prepare_kernel,
        out_shape=pltpu.VMEM((n_tiles, aux_dev * block, 2 * block), BF16),
        in_specs=[pl.BlockSpec(memory_space=pltpu.HBM)],
        out_specs=pl.BlockSpec(memory_space=pltpu.VMEM),
        scratch_shapes=[
            pltpu.VMEM((4, 2, aux_dev, block, block), F32),
            pltpu.SemaphoreType.DMA((4,)),
        ],
        compiler_params=pltpu.CompilerParams(vmem_limit_bytes=24 * MIB),
        cost_estimate=pl.CostEstimate(flops=6 * tiles.size, bytes_accessed=8 * tiles.size, transcendentals=0),
        name="prepare",
    )(pltpu.with_memory_space_constraint(tiles, pltpu.HBM))


def tie(x, *others):
    x, *others = lax.optimization_barrier((x, *others))
    return x, others


class Grid:
    def __init__(self, n_aux):
        self.y, self.core = 2, 2
        self.z = n_aux // (self.y * self.core)
        self.offsets = [(k, j, c) for c in range(self.core) for k in range(self.z) for j in range(self.y)]

    def other(self, me, offset):
        k, j, c = offset
        return me ^ ((k * self.y + j) * self.core + c)

    def shift(self, x, offset):
        return lax.ppermute(x, "aux", [(i, self.other(i, offset)) for i in range(self.z * self.y * self.core)])


def gather_shards(grid, x, beside):
    held = {(0, 0): x}
    held[3, 0] = grid.shift(x, (3, 0, 0))
    held[1, 0] = grid.shift(x, (1, 0, 0))
    held[0, 1] = grid.shift(x, (0, 1, 0))
    held[3, 0], (beside, held[1, 0], held[0, 1]) = tie(held[3, 0], beside, held[1, 0], held[0, 1])

    held[3, 1] = grid.shift(held[3, 0], (0, 1, 0))
    both = grid.shift(jnp.concatenate([held[3, 0], held[0, 1]], axis=0), (1, 0, 0))
    held[2, 1] = grid.shift(held[3, 1], (1, 0, 0))
    groups = {(o,): a for o, a in held.items()}
    groups[(2, 0), (1, 1)] = both

    packs = [[o + (0,) for o in key] for key in groups] + [[o + (1,) for o in key] for key in groups]
    arrays = list(groups.values())
    return packs, arrays + [grid.shift(a, (0, 0, 1)) for a in arrays], beside


def scatter_sums(grid, parts):
    crossed = {k: grid.shift(parts[1][k], (0, 0, 1)) for k in (2, 3, 1, 0)}
    pairs = {k: parts[0][k] + crossed[k] for k in (2, 3, 1, 0)}
    far_away = grid.shift(pairs[2][1], (1, 0, 0))
    far_here, (far_away,) = tie(pairs[2][0], far_away)
    far_here = grid.shift(far_here, (1, 0, 0))
    near = pairs[1][0] + grid.shift(pairs[1][1], (0, 1, 0))
    mirror = grid.shift(pairs[3][1] + far_away, (0, 1, 0))
    own, (mirror,) = tie(pairs[0][1], mirror)
    mirror = pairs[3][0] + far_here + mirror
    own = pairs[0][0] + grid.shift(own, (0, 1, 0))
    return own + grid.shift(near, (1, 0, 0)) + grid.shift(mirror, (3, 0, 0))


def exchange_kernel(grid, per_owner, packs, owner_ref, sub_ref, cols_ref, order_ref, split_ref, *refs):
    n_tiles, rows, pair = split_ref.shape
    block = pair // 2
    aux_dev = rows // block
    shards, refs = refs[: len(packs)], refs[len(packs) :]
    *outs, coeff, wide, fitted, weights, summed = refs
    me = lax.axis_index("aux")
    if grid:
        for ref, offsets in zip(shards, packs):
            for i, offset in enumerate(offsets):
                shard = ref[i * per_owner * block : (i + 1) * per_owner * block]
                coeff[pl.ds(grid.other(me, offset) * per_owner, per_owner)] = shard.reshape(per_owner, block, -1)
    else:
        coeff[...] = shards[0][...].reshape(coeff.shape)

    def position(t):
        return owner_ref[t] * per_owner + sub_ref[t]

    def half_step(t, _):
        c_hi, c_lo = halves(coeff[cols_ref[t]])
        top = jnp.concatenate([c_hi, c_lo], axis=1)
        both = dot(split_ref[t], jnp.concatenate([top, top], axis=0))
        hi, lo = halves(both[:, :block] + both[:, block:])
        for p in range(aux_dev):
            wide[t, :, p * pair : p * pair + block] = hi[p * block : (p + 1) * block]
            wide[t, :, p * pair + block : (p + 1) * pair] = lo[p * block : (p + 1) * block]
        return 0

    lax.fori_loop(0, n_tiles, half_step, 0, unroll=True)
    left, right_hi, right_lo = [], [], []
    for t in range(n_tiles):
        c_hi, c_lo = halves(coeff[order_ref[position(t)]].T)
        left.append(jnp.concatenate([c_hi, c_lo], axis=0))
        w = wide[t]
        right_hi.append(jnp.concatenate([w[:, p * pair : p * pair + block] for p in range(aux_dev)], axis=1))
        right_lo.append(jnp.concatenate([w[:, p * pair + block : (p + 1) * pair] for p in range(aux_dev)], axis=1))
    left = jnp.concatenate(left, axis=1)
    fitted[...] = dot(left, jnp.concatenate(right_hi, axis=0))
    fitted[:block, :] += dot(left[:block], jnp.concatenate(right_lo, axis=0))
    for p in range(aux_dev):
        at = pl.ds(p * block, block)
        f_hi, f_lo = halves((fitted[:block, at] + fitted[block:, at]).T)
        both = jnp.concatenate([f_hi, f_lo], axis=1)
        weights[p * pair : p * pair + block, :] = both
        weights[p * pair + block : (p + 1) * pair, :] = both
    summed[...] = jnp.zeros_like(summed)

    both = dot(wide[...].reshape(n_tiles * block, -1), weights[...])
    value = both[:, :block] + both[:, block:]
    for t in range(n_tiles):
        summed[position(t)] += value[t * block : (t + 1) * block]
    if grid:
        for c in range(grid.core):
            for k in range(grid.z):
                for j in range(grid.y):
                    at = grid.other(me, (k, j, c)) * per_owner
                    outs[c * grid.z + k][j] = summed[pl.ds(at, per_owner)].reshape(outs[0].shape[1:])
    else:
        outs[0][...] = summed[...].reshape(outs[0].shape)


def exchange(grid, tile_owner, tile_sub, tile_cols, row_order, split, packs, shards):
    n_tiles, rows, pair = split.shape
    block, width = pair // 2, shards[0].shape[1]
    aux_dev = rows // block
    n_blocks = row_order.shape[0]
    per_owner = n_blocks // lax.axis_size("aux")
    smem = pl.BlockSpec(memory_space=pltpu.SMEM)
    vmem = pl.BlockSpec(memory_space=pltpu.VMEM)
    if grid:
        out_shape = [pltpu.VMEM((grid.y, per_owner * block, width), F32)] * (grid.core * grid.z)
    else:
        out_shape = [jax.ShapeDtypeStruct((n_blocks * block, width), F32)]
    return pl.pallas_call(
        functools.partial(exchange_kernel, grid, per_owner, packs),
        out_shape=out_shape,
        in_specs=[smem] * 4 + [vmem] * (1 + len(shards)),
        out_specs=[vmem] * len(out_shape),
        scratch_shapes=[
            pltpu.VMEM((n_blocks, block, width), F32),
            pltpu.VMEM((n_tiles, block, aux_dev * pair), BF16),
            pltpu.VMEM((2 * width, aux_dev * block), F32),
            pltpu.VMEM((aux_dev * pair, 2 * width), BF16),
            pltpu.VMEM((n_blocks, block, width), F32),
        ],
        compiler_params=pltpu.CompilerParams(vmem_limit_bytes=(24 if grid else 44) * MIB),
        name="exchange",
    )(tile_owner.reshape(-1), tile_sub, tile_cols, row_order, split, *shards)


def local(tiles, tile_owner, tile_sub, tile_cols, row_order, orbitals):
    n_aux = lax.axis_size("aux")
    grid = Grid(n_aux) if n_aux == 16 else None
    split = prepare(tiles)
    if grid:
        packs, shards, split = gather_shards(grid, orbitals, split)
    else:
        packs, shards = [()], [lax.all_gather(orbitals, "aux", axis=0, tiled=True)]
    split = pltpu.with_memory_space_constraint(split, pltpu.VMEM)
    outs = exchange(grid, tile_owner, tile_sub, tile_cols, row_order, split, packs, shards)
    if not grid:
        return lax.psum_scatter(outs[0], "aux", scatter_dimension=0, tiled=True)
    return scatter_sums(grid, [outs[: grid.z], outs[grid.z :]])


def solution(mesh):
    in_specs = (
        P(("grp", "aux"), None, None, None),
        P(("grp", "aux"), None),
        P(("grp", "aux")),
        P(("grp", "aux")),
        P("grp"),
        P(("grp", "aux"), None),
    )
    out_specs = P(("grp", "aux"), None)
    return jax.shard_map(local, mesh=mesh, in_specs=in_specs, out_specs=out_specs, check_vma=False)
```

```python
import functools

import jax
import jax.numpy as jnp
from jax import lax
from jax.experimental import pallas as pl
from jax.experimental.pallas import tpu as pltpu
from jax.sharding import PartitionSpec as P

F32, BF16 = jnp.float32, jnp.bfloat16
MIB = 1 << 20


def halves(x):
    hi = x.astype(BF16)
    return hi, (x - hi.astype(F32)).astype(BF16)


def dot(a, b):
    return jnp.dot(a, b, preferred_element_type=F32)


def prepare_kernel(tiles_ref, split_ref, buf, sem):
    n_tiles = tiles_ref.shape[0]
    depth, group = buf.shape[0], buf.shape[1]
    steps = n_tiles // group

    def fetch(step, at):
        return pltpu.make_async_copy(tiles_ref.at[pl.ds(step * group, group)], buf.at[at], sem.at[at])

    for step in range(min(depth, steps)):
        fetch(step, step).start()
    for step in range(steps):
        at = step % depth
        fetch(step, at).wait()
        for i in range(group):
            hi, lo = halves(buf[at, i].reshape(-1, buf.shape[-1]))
            split_ref[step * group + i, :, : buf.shape[-1]] = hi
            split_ref[step * group + i, :, buf.shape[-1] :] = lo
        if step + depth < steps:
            fetch(step + depth, at).start()


def prepare(tiles):
    n_tiles, aux_dev, block, _ = tiles.shape
    return pl.pallas_call(
        prepare_kernel,
        out_shape=pltpu.VMEM((n_tiles, aux_dev * block, 2 * block), BF16),
        in_specs=[pl.BlockSpec(memory_space=pltpu.HBM)],
        out_specs=pl.BlockSpec(memory_space=pltpu.VMEM),
        scratch_shapes=[
            pltpu.VMEM((4, 2, aux_dev, block, block), F32),
            pltpu.SemaphoreType.DMA((4,)),
        ],
        compiler_params=pltpu.CompilerParams(vmem_limit_bytes=24 * MIB),
        cost_estimate=pl.CostEstimate(flops=6 * tiles.size, bytes_accessed=8 * tiles.size, transcendentals=0),
        name="prepare",
    )(pltpu.with_memory_space_constraint(tiles, pltpu.HBM))


def tie(x, *others):
    x, *others = lax.optimization_barrier((x, *others))
    return x, others


class Grid:
    def __init__(self, n_aux):
        self.y, self.core = 2, 2
        self.z = n_aux // (self.y * self.core)
        self.offsets = [(k, j, c) for c in range(self.core) for k in range(self.z) for j in range(self.y)]

    def other(self, me, offset):
        k, j, c = offset
        return me ^ ((k * self.y + j) * self.core + c)

    def shift(self, x, offset):
        return lax.ppermute(x, "aux", [(i, self.other(i, offset)) for i in range(self.z * self.y * self.core)])


def gather_shards(grid, x, beside):
    held = {(0, 0): x}
    held[3, 0] = grid.shift(x, (3, 0, 0))
    held[1, 0] = grid.shift(x, (1, 0, 0))
    held[0, 1] = grid.shift(x, (0, 1, 0))
    held[3, 0], (beside, held[1, 0], held[0, 1]) = tie(held[3, 0], beside, held[1, 0], held[0, 1])

    held[3, 1] = grid.shift(held[3, 0], (0, 1, 0))
    both = grid.shift(jnp.concatenate([held[3, 0], held[0, 1]], axis=0), (1, 0, 0))
    held[2, 1] = grid.shift(held[3, 1], (1, 0, 0))
    groups = {(o,): a for o, a in held.items()}
    groups[(2, 0), (1, 1)] = both

    packs = [[o + (0,) for o in key] for key in groups] + [[o + (1,) for o in key] for key in groups]
    arrays = list(groups.values())
    return packs, arrays + [grid.shift(a, (0, 0, 1)) for a in arrays], beside


def scatter_sums(grid, parts):
    crossed = {k: grid.shift(parts[1][k], (0, 0, 1)) for k in (2, 3, 1, 0)}
    pairs = {k: parts[0][k] + crossed[k] for k in (2, 3, 1, 0)}
    far_away = grid.shift(pairs[2][1], (1, 0, 0))
    near = pairs[1][0] + grid.shift(pairs[1][1], (0, 1, 0))
    mirror = grid.shift(pairs[3][1] + far_away, (0, 1, 0))
    both = grid.shift(jnp.concatenate([pairs[2][0], near], axis=0), (1, 0, 0))
    far_here, near = both[: near.shape[0]], both[near.shape[0] :]
    own, (mirror,) = tie(pairs[0][1], mirror)
    mirror = pairs[3][0] + far_here + mirror
    own = pairs[0][0] + grid.shift(own, (0, 1, 0))
    return own + near + grid.shift(mirror, (3, 0, 0))


def exchange_kernel(grid, per_owner, packs, owner_ref, sub_ref, cols_ref, order_ref, split_ref, *refs):
    n_tiles, rows, pair = split_ref.shape
    block = pair // 2
    aux_dev = rows // block
    shards, refs = refs[: len(packs)], refs[len(packs) :]
    *outs, coeff, wide, fitted, weights, summed = refs
    me = lax.axis_index("aux")
    if grid:
        for ref, offsets in zip(shards, packs):
            for i, offset in enumerate(offsets):
                shard = ref[i * per_owner * block : (i + 1) * per_owner * block]
                coeff[pl.ds(grid.other(me, offset) * per_owner, per_owner)] = shard.reshape(per_owner, block, -1)
    else:
        coeff[...] = shards[0][...].reshape(coeff.shape)

    def position(t):
        return owner_ref[t] * per_owner + sub_ref[t]

    def half_step(t, _):
        c_hi, c_lo = halves(coeff[cols_ref[t]])
        top = jnp.concatenate([c_hi, c_lo], axis=1)
        both = dot(split_ref[t], jnp.concatenate([top, top], axis=0))
        hi, lo = halves(both[:, :block] + both[:, block:])
        for p in range(aux_dev):
            wide[t, :, p * pair : p * pair + block] = hi[p * block : (p + 1) * block]
            wide[t, :, p * pair + block : (p + 1) * pair] = lo[p * block : (p + 1) * block]
        return 0

    lax.fori_loop(0, n_tiles, half_step, 0, unroll=True)
    left, right_hi, right_lo = [], [], []
    for t in range(n_tiles):
        c_hi, c_lo = halves(coeff[order_ref[position(t)]].T)
        left.append(jnp.concatenate([c_hi, c_lo], axis=0))
        w = wide[t]
        right_hi.append(jnp.concatenate([w[:, p * pair : p * pair + block] for p in range(aux_dev)], axis=1))
        right_lo.append(jnp.concatenate([w[:, p * pair + block : (p + 1) * pair] for p in range(aux_dev)], axis=1))
    left = jnp.concatenate(left, axis=1)
    fitted[...] = dot(left, jnp.concatenate(right_hi, axis=0))
    fitted[:block, :] += dot(left[:block], jnp.concatenate(right_lo, axis=0))
    for p in range(aux_dev):
        at = pl.ds(p * block, block)
        f_hi, f_lo = halves((fitted[:block, at] + fitted[block:, at]).T)
        both = jnp.concatenate([f_hi, f_lo], axis=1)
        weights[p * pair : p * pair + block, :] = both
        weights[p * pair + block : (p + 1) * pair, :] = both
    summed[...] = jnp.zeros_like(summed)

    both = dot(wide[...].reshape(n_tiles * block, -1), weights[...])
    value = both[:, :block] + both[:, block:]
    for t in range(n_tiles):
        summed[position(t)] += value[t * block : (t + 1) * block]
    if grid:
        for c in range(grid.core):
            for k in range(grid.z):
                for j in range(grid.y):
                    at = grid.other(me, (k, j, c)) * per_owner
                    outs[c * grid.z + k][j] = summed[pl.ds(at, per_owner)].reshape(outs[0].shape[1:])
    else:
        outs[0][...] = summed[...].reshape(outs[0].shape)


def exchange(grid, tile_owner, tile_sub, tile_cols, row_order, split, packs, shards):
    n_tiles, rows, pair = split.shape
    block, width = pair // 2, shards[0].shape[1]
    aux_dev = rows // block
    n_blocks = row_order.shape[0]
    per_owner = n_blocks // lax.axis_size("aux")
    smem = pl.BlockSpec(memory_space=pltpu.SMEM)
    vmem = pl.BlockSpec(memory_space=pltpu.VMEM)
    if grid:
        out_shape = [pltpu.VMEM((grid.y, per_owner * block, width), F32)] * (grid.core * grid.z)
    else:
        out_shape = [jax.ShapeDtypeStruct((n_blocks * block, width), F32)]
    return pl.pallas_call(
        functools.partial(exchange_kernel, grid, per_owner, packs),
        out_shape=out_shape,
        in_specs=[smem] * 4 + [vmem] * (1 + len(shards)),
        out_specs=[vmem] * len(out_shape),
        scratch_shapes=[
            pltpu.VMEM((n_blocks, block, width), F32),
            pltpu.VMEM((n_tiles, block, aux_dev * pair), BF16),
            pltpu.VMEM((2 * width, aux_dev * block), F32),
            pltpu.VMEM((aux_dev * pair, 2 * width), BF16),
            pltpu.VMEM((n_blocks, block, width), F32),
        ],
        compiler_params=pltpu.CompilerParams(vmem_limit_bytes=(24 if grid else 44) * MIB),
        name="exchange",
    )(tile_owner.reshape(-1), tile_sub, tile_cols, row_order, split, *shards)


def local(tiles, tile_owner, tile_sub, tile_cols, row_order, orbitals):
    n_aux = lax.axis_size("aux")
    grid = Grid(n_aux) if n_aux == 16 else None
    split = prepare(tiles)
    if grid:
        packs, shards, split = gather_shards(grid, orbitals, split)
    else:
        packs, shards = [()], [lax.all_gather(orbitals, "aux", axis=0, tiled=True)]
    split = pltpu.with_memory_space_constraint(split, pltpu.VMEM)
    outs = exchange(grid, tile_owner, tile_sub, tile_cols, row_order, split, packs, shards)
    if not grid:
        return lax.psum_scatter(outs[0], "aux", scatter_dimension=0, tiled=True)
    return scatter_sums(grid, [outs[: grid.z], outs[grid.z :]])


def solution(mesh):
    in_specs = (
        P(("grp", "aux"), None, None, None),
        P(("grp", "aux"), None),
        P(("grp", "aux")),
        P(("grp", "aux")),
        P("grp"),
        P(("grp", "aux"), None),
    )
    out_specs = P(("grp", "aux"), None)
    return jax.shard_map(local, mesh=mesh, in_specs=in_specs, out_specs=out_specs, check_vma=False)
```
